32 devices in a mesh: row: 4 (over y, x), col: 4 (over z), rep: 2 (over core).
Axes of the slice: x: 2, y: 2, z: 4, core: 2. Of those that a mesh axis runs over, the one named last changes fastest.
Arguments:
- patches: bfloat16 [2, 256, 6144], P('rep', 'col', 'row'), may hold values from -6 to 6
- cotangent: bfloat16 [2, 256, 6144], P('rep', 'col', 'row'), may hold values from -6 to 6
- w_in: bfloat16 [6144, 24576], P('row', 'col'), may hold values from -0.078125 to 0.078125
- w_out: bfloat16 [24576, 6144], P('col', 'row'), may hold values from -0.0390625 to 0.0390625
- moment_in: bfloat16 [2, 6144, 24576], P('rep', 'row', 'col'), may hold values from -2 to 2
- moment_out: bfloat16 [2, 24576, 6144], P('rep', 'col', 'row'), may hold values from -2 to 2
Outputs:
- mixed: bfloat16 [2, 256, 6144], P('rep', 'col', 'row')
- tally_in: bfloat16 [6144, 24576], P('row', 'col')
- tally_out: bfloat16 [24576, 6144], P('col', 'row')
The draws below stay inside these ranges and needn't reach their ends.
All inputs are finite; a program needn't handle non-finite values.
Results may differ from the reference program's by a relative error of at most 0.0055.
Values may be sent and summed in bfloat16 or wider, within the bound.
No kernel may reach another device: no remote copies, remote signals or barrier semaphores. Data moves between devices by JAX's collectives and lax.ppermute only.
A program may use at most 256 MiB of HBM per device.

```python
import math
import jax
import jax.numpy as jnp
from jax import lax

D = 6144
FF = 24576
TOK_REP = 256
REPS = 2
N_REP = 2


def levels(key, extent, split, low, high):
    gain, own = 1.0, jax.random.fold_in(key, 6)
    for dim, parts in split:
        heights = jnp.exp(jax.random.uniform(jax.random.fold_in(own, dim), (parts,), jnp.float32, low / len(split), high / len(split)))
        gain = gain * jnp.repeat(heights, extent[dim] // parts).reshape([-1 if axis == dim else 1 for axis in range(len(extent))])
    return gain


def scatter_about(rng, dims, scale, reach, cuts=(), kind=jnp.bfloat16):
    values = scale * jax.random.normal(rng, dims, jnp.float32)
    if cuts:
        values = values * levels(rng, dims, cuts, -0.22, 0.18)
    return jnp.clip(values, -reach, reach).astype(kind)


def setup_inputs(seed: int = 0) -> dict:
    key_of = jax.random.split(jax.random.key(seed), 7)
    return {
        "patches": scatter_about(key_of[0], (REPS, TOK_REP, D), 1.0, 6.0, ((0, 2), (1, 4), (2, 4))),
        "cotangent": scatter_about(key_of[1], (REPS, TOK_REP, D), 1.0, 6.0, ((0, 2), (1, 4), (2, 4))),
        "w_in": scatter_about(key_of[2], (D, FF), D ** -0.5, 0.078125, ((0, 4), (1, 4))),
        "w_out": scatter_about(key_of[3], (FF, D), FF ** -0.5, 0.0390625, ((0, 4), (1, 4))),
        "moment_in": scatter_about(key_of[4], (REPS, D, FF), 0.3, 2.0, ((0, 2), (1, 4), (2, 4))),
        "moment_out": scatter_about(key_of[5], (REPS, FF, D), 0.3, 2.0, ((0, 2), (1, 4), (2, 4))),
    }


momentum_decay = 0.9
vote_scale = 0.3

def gelu_value(pre):
    return 0.5 * pre * (1.0 + lax.erf(pre * (1.0 / math.sqrt(2.0))))

def gelu_slope(pre):
    return 0.5 * (1.0 + lax.erf(pre * (1.0 / math.sqrt(2.0)))) + pre * jnp.exp(-0.5 * pre * pre) * (1.0 / math.sqrt(2.0 * math.pi))

def reference(patches, cotangent, w_in, w_out, moment_in, moment_out):
    norm_factor = 1.0 / math.sqrt(TOK_REP)
    tally_first = jnp.zeros((D, FF), jnp.float32)
    tally_second = jnp.zeros((FF, D), jnp.float32)
    outputs = []
    for replica in range(N_REP):
        inputs = patches[replica]
        grads = cotangent[replica]
        pre = jnp.dot(inputs, w_in, preferred_element_type=jnp.float32)
        hidden = gelu_value(pre).astype(jnp.bfloat16)
        outputs.append(jnp.dot(hidden, w_out, preferred_element_type=jnp.float32).astype(jnp.bfloat16))
        back = lax.dot_general(grads, w_out, (((1,), (1,)), ((), ())), preferred_element_type=jnp.float32)
        slope = (back * gelu_slope(pre)).astype(jnp.bfloat16)
        grad_first = lax.dot_general(inputs, slope, (((0,), (0,)), ((), ())), preferred_element_type=jnp.float32) * norm_factor
        grad_second = lax.dot_general(hidden, grads, (((0,), (0,)), ((), ())), preferred_element_type=jnp.float32) * norm_factor
        moved_first = momentum_decay * moment_in[replica].astype(jnp.float32) + (1.0 - momentum_decay) * grad_first
        moved_second = momentum_decay * moment_out[replica].astype(jnp.float32) + (1.0 - momentum_decay) * grad_second
        tally_first = tally_first + jnp.tanh(moved_first / vote_scale).astype(jnp.bfloat16).astype(jnp.float32)
        tally_second = tally_second + jnp.tanh(moved_second / vote_scale).astype(jnp.bfloat16).astype(jnp.float32)
    mixed = jnp.stack(outputs, axis=0)
    return (mixed, tally_first.astype(jnp.bfloat16), tally_second.astype(jnp.bfloat16))
```

```python
import functools
import math

import jax
import jax.numpy as jnp
from jax import lax
from jax.experimental import pallas as pl
from jax.experimental.pallas import tpu as pltpu
from jax.sharding import PartitionSpec as P

momentum_decay = 0.9
vote_scale = 0.3
vmem_bytes = 48 * 2**20
hbm = pl.BlockSpec(memory_space=pl.ANY)


def cost(flops, moved, transcendentals=0):
    return pl.CostEstimate(
        flops=int(flops), bytes_accessed=int(moved), transcendentals=int(transcendentals)
    )


def gelu_value(pre):
    return 0.5 * pre * (1.0 + lax.erf(pre * (1.0 / math.sqrt(2.0))))


def gelu_slope(pre):
    return 0.5 * (1.0 + lax.erf(pre * (1.0 / math.sqrt(2.0)))) + pre * jnp.exp(-0.5 * pre * pre) * (
        1.0 / math.sqrt(2.0 * math.pi)
    )


def shards_plain(patches, cotangent, w_in, w_out, moment_in, moment_out):
    inputs = lax.all_gather(patches[0], "col", axis=0, tiled=True)
    norm_factor = 1.0 / math.sqrt(inputs.shape[0])
    pre_share = lax.psum_scatter(
        jnp.dot(inputs, w_in, preferred_element_type=jnp.float32),
        "row",
        scatter_dimension=0,
        tiled=True,
    )
    hidden = lax.all_gather(
        gelu_value(pre_share).astype(jnp.bfloat16), "row", axis=0, tiled=True
    )
    mixed = lax.psum_scatter(
        jnp.dot(hidden, w_out, preferred_element_type=jnp.float32),
        "col",
        scatter_dimension=0,
        tiled=True,
    ).astype(jnp.bfloat16)
    grads = lax.all_gather(cotangent[0], "col", axis=0, tiled=True)
    back_share = lax.psum_scatter(
        lax.dot_general(
            grads, w_out, (((1,), (1,)), ((), ())), preferred_element_type=jnp.float32
        ).astype(jnp.bfloat16),
        "row",
        scatter_dimension=0,
        tiled=True,
    ).astype(jnp.float32)
    slope_share = (back_share * gelu_slope(pre_share)).astype(jnp.bfloat16)
    slope = lax.all_gather(slope_share, "row", axis=0, tiled=True)

    def votes(moment, left, right):
        grad = norm_factor * lax.dot_general(
            left, right, (((0,), (0,)), ((), ())), preferred_element_type=jnp.float32
        )
        moved = momentum_decay * moment.astype(jnp.float32) + (1.0 - momentum_decay) * grad
        vote = jnp.tanh(moved / vote_scale).astype(jnp.bfloat16)
        return lax.psum(vote, "rep").astype(jnp.float32).astype(jnp.bfloat16)

    return (
        mixed[None],
        votes(moment_in[0], inputs, slope),
        votes(moment_out[0], hidden, grads),
    )


def project_body(transposed, n_tok, idx, *refs):
    toks, w, (send_a, keep_a, send_b, keep_b, whole) = refs[:n_tok], refs[n_tok], refs[-5:]
    step = pl.program_id(0)

    @pl.when(step == 0)
    def _():
        for b, t in enumerate(toks):
            whole[b * t.shape[0] : (b + 1) * t.shape[0]] = t[...]

    contract = ((1,), (1,)) if transposed else ((1,), (0,))
    out = lax.dot_general(
        whole[...], w[...], (contract, ((), ())), preferred_element_type=jnp.float32
    )
    places = (
        (keep_a, 0), (keep_b, 0),
        (send_a, 0), (keep_b, 1),
        (keep_a, 1), (send_b, 0),
        (send_a, 1), (send_b, 1),
    )
    for at, (ref, slot) in enumerate(places):
        @pl.when(step == at)
        def _():
            ref[slot] = out.astype(ref.dtype)


def project(me, toks, w, transposed, n_row, after=()):
    rows = sum(t.shape[0] for t in toks)
    depth = toks[0].shape[1]
    wide = (w.shape[0] if transposed else w.shape[1]) // (2 * n_row)

    def block(s, idx):
        return ((idx[0] ^ (s // 2)) * 2 + s % 2, 0)

    if transposed:
        w_spec = pl.BlockSpec((wide, depth), block)
    else:
        w_spec = pl.BlockSpec((depth, wide), lambda s, idx: block(s, idx)[::-1])
    send = jax.ShapeDtypeStruct((2, rows, wide), jnp.bfloat16)
    keep = jax.ShapeDtypeStruct((2, rows, wide), jnp.float32)
    whole = jax.ShapeDtypeStruct((rows, depth), jnp.bfloat16)
    return pl.pallas_call(
        functools.partial(project_body, transposed, len(toks)),
        grid_spec=pltpu.PrefetchScalarGridSpec(
            num_scalar_prefetch=1,
            grid=(2 * n_row,),
            in_specs=[pl.BlockSpec(t.shape, lambda s, idx: (0, 0)) for t in toks]
            + [w_spec] + [hbm] * len(after),
            out_specs=[pl.BlockSpec(send.shape, lambda s, idx: (0, 0, 0))] * 4
            + [pl.BlockSpec(whole.shape, lambda s, idx: (0, 0))],
        ),
        out_shape=[send, keep, send, keep, whole],
        compiler_params=pltpu.CompilerParams(vmem_limit_bytes=vmem_bytes),
        cost_estimate=cost(2 * rows * w.size, 2 * w.size + 2 * rows * depth + 24 * rows * wide),
        name="project_back" if transposed else "project_pre",
    )(me, *toks, w, *after)


def mix_body(n_half, n_col, n_after, idx, *refs):
    hidden, w = refs[:n_half], refs[n_half]
    out, pack, total = refs[-3:]
    step = pl.program_id(0)
    for at, h in enumerate(hidden):
        @pl.when(step == at)
        def _():
            part = jnp.dot(h[...], w[...], preferred_element_type=jnp.float32)
            total[...] = part if at == 0 else total[...] + part
            if at >= 2:
                pack[at - 2] = h[...]
    @pl.when(step == n_half - 1)
    def _():
        rows = out.shape[1]
        for b in range(n_col):
            out[lax.rem(idx[1] + n_col - b, n_col)] = total[b * rows : (b + 1) * rows]


def half_spec(whole, h):
    if whole.ndim == 3:
        return pl.BlockSpec((None,) + whole.shape[1:], lambda *_: (h, 0, 0))
    return pl.BlockSpec(whole.shape, lambda *_: (0, 0))


def mix(at, halves, w, n_col, after=()):
    rows, wide = halves[0][0].shape[-2:]
    depth = w.shape[1]
    share = rows // n_col
    n_half = len(halves)
    out = jax.ShapeDtypeStruct((n_col, share, depth), jnp.float32)
    pack = jax.ShapeDtypeStruct((n_half - 2, rows, wide), jnp.bfloat16)
    return pl.pallas_call(
        functools.partial(mix_body, n_half, n_col, len(after)),
        grid_spec=pltpu.PrefetchScalarGridSpec(
            num_scalar_prefetch=1,
            grid=(n_half,),
            in_specs=[half_spec(*h) for h in halves]
            + [pl.BlockSpec((wide, depth), lambda s, idx: ((idx[0] ^ (s // 2)) * 2 + s % 2, 0))]
            + [hbm] * len(after),
            out_specs=[pl.BlockSpec(a.shape, lambda s, idx: (0, 0, 0)) for a in (out, pack)],
            scratch_shapes=[pltpu.VMEM((rows, depth), jnp.float32)],
        ),
        out_shape=[out, pack],
        compiler_params=pltpu.CompilerParams(vmem_limit_bytes=vmem_bytes),
        cost_estimate=cost(2 * rows * w.size, 2 * w.size + 4 * rows * w.shape[0] + 4 * rows * depth),
        name="mix",
    )(at, *[h[0] for h in halves], w, *after)


def late_body(keep_a, got_a, keep_b, got_b, *refs):
    out_a, out_b = refs[-2:]
    for keep, got, out in ((keep_a, got_a, out_a), (keep_b, got_b, out_b)):
        out[...] = (keep[...] + got[...].astype(jnp.float32)).astype(jnp.bfloat16)


def late_sums(keep_a, got_a, keep_b, got_b, after):
    _, rows, wide = keep_a.shape
    spec = pl.BlockSpec((None, rows, wide), lambda i: (1, 0, 0))
    out = jax.ShapeDtypeStruct((rows, wide), jnp.bfloat16)
    return pl.pallas_call(
        late_body,
        grid=(1,),
        in_specs=[spec] * 4 + [hbm] * len(after),
        out_specs=[pl.BlockSpec((rows, wide), lambda i: (0, 0))] * 2,
        out_shape=[out, out],
        compiler_params=pltpu.CompilerParams(vmem_limit_bytes=vmem_bytes),
        name="late_sums",
    )(keep_a, got_a, keep_b, got_b, *after)


def sum_of(keep_a, got_a, late_a, keep_b, got_b, late_b):
    return [
        (0, keep_a[...] + got_a[...].astype(jnp.float32) + late_a[...].astype(jnp.float32)),
        (1, keep_b[...] + got_b[...].astype(jnp.float32) + late_b[...].astype(jnp.float32)),
    ]


def hidden_body(*refs):
    tokens, (hidden, pack, steep) = refs[6], refs[-3:]
    wide = hidden.shape[2]
    for h, pre in sum_of(*refs[:6]):
        value = gelu_value(pre).astype(jnp.bfloat16)
        hidden[h] = pack[h] = value
        pack[2 + h] = tokens[:, h * wide : (h + 1) * wide]
        steep[h] = gelu_slope(pre)


def slope_body(*refs):
    tokens, steep, (slope, pack) = refs[6], refs[7], refs[-2:]
    wide = slope.shape[2]
    for h, back in sum_of(*refs[:6]):
        value = (back * steep[h]).astype(jnp.bfloat16)
        slope[h] = pack[h] = value
        pack[2 + h] = tokens[:, h * wide : (h + 1) * wide]


def finish(body, name, kinds, parts, tokens, more=(), after=()):
    _, rows, wide = parts[0].shape
    kept = pl.BlockSpec((None, rows, wide), lambda i: (0, 0, 0))
    late = pl.BlockSpec((rows, wide), lambda i: (0, 0))
    full = pl.BlockSpec((2, rows, wide), lambda i: (0, 0, 0))
    return pl.pallas_call(
        body,
        grid=(1,),
        in_specs=[kept, kept, late] * 2 + [pl.BlockSpec(tokens.shape, lambda i: (0, 0))]
        + [full] * len(more) + [hbm] * len(after),
        out_specs=[pl.BlockSpec((n, rows, wide), lambda i: (0, 0, 0)) for n, _ in kinds],
        out_shape=[jax.ShapeDtypeStruct((n, rows, wide), k) for n, k in kinds],
        compiler_params=pltpu.CompilerParams(vmem_limit_bytes=vmem_bytes),
        name=name,
    )(*parts, tokens, *more, *after)


def forward_body(from_x, from_y, *refs):
    out_a, out_b = refs[-2:]
    out_a[...] = from_x[...]
    out_b[...] = from_y[...]


def forward(from_x, from_y, after):
    _, rows, wide = from_x.shape
    out = jax.ShapeDtypeStruct((rows, wide), jnp.bfloat16)
    return pl.pallas_call(
        forward_body,
        grid=(1,),
        in_specs=[pl.BlockSpec((None, rows, wide), lambda i, h=h: (h, 0, 0)) for h in range(2)]
        + [hbm] * len(after),
        out_specs=[pl.BlockSpec((rows, wide), lambda i: (0, 0))] * 2,
        out_shape=[out, out],
        compiler_params=pltpu.CompilerParams(vmem_limit_bytes=vmem_bytes),
        name="forward",
    )(from_x, from_y, *after)


def vote_of(grad, moment, scale):
    moved = (momentum_decay / vote_scale) * moment.astype(jnp.float32) + scale * grad
    return jnp.tanh(moved).astype(jnp.bfloat16)


def transposed_dot(left, right):
    return lax.dot_general(
        left, right, (((0,), (0,)), ((), ())), preferred_element_type=jnp.float32
    )


def total_of(first, second):
    return first + second


def tally_in_body(scale, idx, x0, x1, s0, s1, m0, m1, *rest):
    out = rest[-1]
    wide = s0.shape[2]
    for h in range(2):
        for c in range(0, wide, wide // 2):
            part = slice(c, c + wide // 2)
            to = slice(h * wide + c, h * wide + c + wide // 2)
            v0 = vote_of(transposed_dot(x0[...], s0[h, :, part]), m0[:, to], scale)
            v1 = vote_of(transposed_dot(x1[...], s1[h, :, part]), m1[:, to], scale)
            out[:, to] = total_of(v0, v1)


def tally_out_body(scale, idx, c0, c1, s0, s1, m0, m1, *rest):
    out = rest[-1]
    half = c1.shape[2]
    step = half // 2 if half % 256 == 0 else half
    for h in range(2):
        for c in range(0, half, step):
            part = slice(c, c + step)
            to = slice(h * half + c, h * half + c + step)
            v0 = vote_of(transposed_dot(s0[...], c0[:, to]), m0[:, to], scale)
            v1 = vote_of(transposed_dot(s1[...], c1[h, :, part]), m1[:, to], scale)
            out[:, to] = total_of(v0, v1)


def tally(kind, quarters, fixed, halves, moments, into, scale, after=()):
    rows, cols = moments[0].shape
    n_half, (_, toks, wide) = 2 * (quarters.size - 1), halves[0].shape
    if kind == "in":
        high = 256 if wide % 256 == 0 else wide
        grid = (n_half // 2, rows // high)
        per = wide // high
        fixed_specs = [
            pl.BlockSpec((toks, high), lambda k, i, q: (0, i)),
            pl.BlockSpec((None, toks, high), lambda k, i, q: (2 + i // per, 0, i % per)),
        ]
        pair_spec = pl.BlockSpec((2, toks, wide), lambda k, i, q: (k, 0, 0))
        m_spec = pl.BlockSpec((high, 2 * wide), lambda k, i, q: (i, q[k]))
        peer_spec = pl.BlockSpec((None, high, 2 * wide), lambda k, i, q: (q[n_half // 2], i, q[k]))
        body = functools.partial(tally_in_body, scale)
        area = rows * n_half * wide
    else:
        high = 256 if wide % 256 == 0 else wide
        per = wide // high
        grid = (n_half // 2, 2, per)
        fixed_specs = [
            pl.BlockSpec((toks, cols), lambda k, h, i, q: (0, 0)),
            pl.BlockSpec((2, toks, wide), lambda k, h, i, q: (1, 0, 0)),
        ]
        pair_spec = pl.BlockSpec((None, toks, high), lambda k, h, i, q: (2 * k + h, 0, i))
        m_spec = pl.BlockSpec((high, cols), lambda k, h, i, q: ((2 * q[k] + h) * per + i, 0))
        peer_spec = pl.BlockSpec(
            (None, high, cols), lambda k, h, i, q: (q[n_half // 2], (2 * q[k] + h) * per + i, 0)
        )
        body = functools.partial(tally_out_body, scale)
        area = cols * n_half * wide
    old = [] if into is None else [into]
    return pl.pallas_call(
        body,
        grid_spec=pltpu.PrefetchScalarGridSpec(
            num_scalar_prefetch=1,
            grid=grid,
            in_specs=fixed_specs + [pair_spec] * 2
            + [m_spec, peer_spec if moments[1].ndim == 3 else m_spec]
            + [hbm] * len(old + list(after)),
            out_specs=m_spec,
        ),
        out_shape=jax.ShapeDtypeStruct((rows, cols), jnp.bfloat16),
        input_output_aliases={7: 0} if old else {},
        compiler_params=pltpu.CompilerParams(vmem_limit_bytes=vmem_bytes),
        cost_estimate=cost(4 * toks * area, 6 * area, 2 * area),
        name="tally_" + kind,
    )(quarters, *fixed, *halves, *moments, *old, *after)


def shards_square(n_col, n_rep, patches, cotangent, w_in, w_out, moment_in, moment_out):
    n_row = 4
    across_x = [(i, i ^ 1) for i in range(n_row)]
    across_y = [(i, i ^ 2) for i in range(n_row)]
    swap = [(0, 1), (1, 0)]
    row_index = lax.axis_index("row")
    me = jnp.reshape(row_index, (1,)).astype(jnp.int32)

    def to_x(a):
        return lax.ppermute(a, "row", across_x)

    def to_y(a):
        return lax.ppermute(a, "row", across_y)

    def other(a):
        return lax.ppermute(a, "rep", swap)

    def along(a, shift):
        return lax.ppermute(a, "col", [(i, (i + shift) % n_col) for i in range(n_col)])

    def f32(a):
        return a.astype(jnp.float32)

    peer = 1 - jnp.reshape(lax.axis_index("rep"), (1,)).astype(jnp.int32)

    def quarters(*ks):
        return jnp.concatenate([me ^ k for k in ks] + [peer])

    own_x, own_c = patches[0], cotangent[0]
    moment_in, moment_out = moment_in[0], moment_out[0]

    xs = [own_x] + [along(own_x, b) for b in range(1, n_col)]
    cs = [own_c] + [along(own_c, b) for b in range(1, n_col)]
    every_moment_out = lax.all_gather(moment_out, "rep")
    every_moment_in = lax.all_gather(moment_in, "rep")

    send_a, pre_a, send_b, pre_b, x_all = project(me, xs, w_in, False, n_row)
    pre_got_a, pre_got_b = to_x(send_a), to_y(send_b)
    send_a, back_a, send_b, back_b, c_all = project(me, cs, w_out, True, n_row, after=(x_all,))
    back_got_a, back_got_b = to_x(send_a), to_y(send_b)
    scale = (1.0 - momentum_decay) / (vote_scale * math.sqrt(x_all.shape[0]))

    late_a, late_b = late_sums(pre_a, pre_got_a, pre_b, pre_got_b, after=(c_all,))
    pre_late_a, pre_late_b = to_y(late_a), to_x(late_b)
    late_a, late_b = late_sums(back_a, back_got_a, back_b, back_got_b, after=(late_a,))
    back_late_a, back_late_b = to_y(late_a), to_x(late_b)

    bf16 = jnp.bfloat16
    hidden, pack, steep = finish(
        hidden_body, "hidden", ((2, bf16), (4, bf16), (2, jnp.float32)),
        (pre_a, pre_got_a, pre_late_a, pre_b, pre_got_b, pre_late_b), c_all, after=(late_a,),
    )
    hidden_x, hidden_y, hidden_other = to_x(hidden), to_y(hidden), other(pack)
    slope, pack = finish(
        slope_body, "slope", ((2, bf16), (4, bf16)),
        (back_a, back_got_a, back_late_a, back_b, back_got_b, back_late_b), x_all, (steep,),
    )
    slope_x, slope_y, slope_other = to_x(slope), to_y(slope), other(pack)

    both_c, both_out = (c_all, hidden_other), (moment_out, every_moment_out)
    both_x, both_in = (x_all, slope_other), (moment_in, every_moment_in)

    tally_out = tally(
        "out", quarters(0), both_c, (hidden, hidden_other), both_out, None, scale, after=(slope,)
    )
    near_a, near_b = forward(hidden_x, hidden_y, after=(tally_out,))
    hidden_far_a, hidden_far_b = to_y(near_a), to_x(near_b)
    far_a, far_b = forward(slope_x, slope_y, after=(near_a,))
    tally_in = tally(
        "in", quarters(0), both_x, (slope, slope_other), both_in, None, scale, after=(far_a,)
    )
    slope_far_a, slope_far_b = to_y(far_a), to_x(far_b)
    column = jnp.reshape(lax.axis_index("col"), (1,)).astype(jnp.int32)
    parts, hidden_rest = mix(
        jnp.concatenate([me, column]),
        [(a, h) for a in (hidden, hidden_x, hidden_y) for h in range(2)]
        + [(hidden_far_a, 0), (hidden_far_b, 0)],
        w_out,
        n_col,
        after=(tally_in, slope_far_a, slope_far_b),
    )
    mixed = lax.psum_scatter(parts, "col", scatter_dimension=0, tiled=True).astype(bf16)
    hidden_rest_other = other(hidden_rest)
    near = jnp.concatenate([slope_x, slope_y])
    near_other = other(near)
    tally_out = tally(
        "out", quarters(1, 2, 3), both_c, (hidden_rest, hidden_rest_other), both_out, tally_out,
        scale, after=(near, far_a),
    )
    tally_in = tally(
        "in", quarters(1, 2), both_x, (near, near_other), both_in, tally_in, scale,
        after=(tally_out,),
    )
    far = jnp.stack([slope_far_a, slope_far_b])
    tally_in = tally("in", quarters(3), both_x, (far, other(far)), both_in, tally_in, scale)
    return mixed, tally_in, tally_out


def solution(mesh):
    in_specs = (
        P("rep", "col", "row"),
        P("rep", "col", "row"),
        P("row", "col"),
        P("col", "row"),
        P("rep", "row", "col"),
        P("rep", "col", "row"),
    )
    out_specs = (P("rep", "col", "row"), P("row", "col"), P("col", "row"))
    sizes = dict(mesh.shape)
    if sizes["row"] == 4 and sizes["rep"] == 2:
        body = functools.partial(shards_square, sizes["col"], sizes["rep"])
    else:
        body = shards_plain
    return jax.shard_map(body, mesh=mesh, in_specs=in_specs, out_specs=out_specs, check_vma=False)
```

```python
import functools
import math

import jax
import jax.numpy as jnp
from jax import lax
from jax.experimental import pallas as pl
from jax.experimental.pallas import tpu as pltpu
from jax.sharding import PartitionSpec as P

momentum_decay = 0.9
vote_scale = 0.3
vmem_bytes = 48 * 2**20
hbm = pl.BlockSpec(memory_space=pl.ANY)


def cost(flops, moved, transcendentals=0):
    return pl.CostEstimate(
        flops=int(flops), bytes_accessed=int(moved), transcendentals=int(transcendentals)
    )


def gelu_value(pre):
    return 0.5 * pre * (1.0 + lax.erf(pre * (1.0 / math.sqrt(2.0))))


def gelu_slope(pre):
    return 0.5 * (1.0 + lax.erf(pre * (1.0 / math.sqrt(2.0)))) + pre * jnp.exp(-0.5 * pre * pre) * (
        1.0 / math.sqrt(2.0 * math.pi)
    )


def shards_plain(patches, cotangent, w_in, w_out, moment_in, moment_out):
    inputs = lax.all_gather(patches[0], "col", axis=0, tiled=True)
    norm_factor = 1.0 / math.sqrt(inputs.shape[0])
    pre_share = lax.psum_scatter(
        jnp.dot(inputs, w_in, preferred_element_type=jnp.float32),
        "row",
        scatter_dimension=0,
        tiled=True,
    )
    hidden = lax.all_gather(
        gelu_value(pre_share).astype(jnp.bfloat16), "row", axis=0, tiled=True
    )
    mixed = lax.psum_scatter(
        jnp.dot(hidden, w_out, preferred_element_type=jnp.float32),
        "col",
        scatter_dimension=0,
        tiled=True,
    ).astype(jnp.bfloat16)
    grads = lax.all_gather(cotangent[0], "col", axis=0, tiled=True)
    back_share = lax.psum_scatter(
        lax.dot_general(
            grads, w_out, (((1,), (1,)), ((), ())), preferred_element_type=jnp.float32
        ).astype(jnp.bfloat16),
        "row",
        scatter_dimension=0,
        tiled=True,
    ).astype(jnp.float32)
    slope_share = (back_share * gelu_slope(pre_share)).astype(jnp.bfloat16)
    slope = lax.all_gather(slope_share, "row", axis=0, tiled=True)

    def votes(moment, left, right):
        grad = norm_factor * lax.dot_general(
            left, right, (((0,), (0,)), ((), ())), preferred_element_type=jnp.float32
        )
        moved = momentum_decay * moment.astype(jnp.float32) + (1.0 - momentum_decay) * grad
        vote = jnp.tanh(moved / vote_scale).astype(jnp.bfloat16)
        return lax.psum(vote, "rep").astype(jnp.float32).astype(jnp.bfloat16)

    return (
        mixed[None],
        votes(moment_in[0], inputs, slope),
        votes(moment_out[0], hidden, grads),
    )


def project_body(transposed, n_tok, idx, *refs):
    toks, w, (send_a, keep_a, send_b, keep_b, whole) = refs[:n_tok], refs[n_tok], refs[-5:]
    step = pl.program_id(0)

    @pl.when(step == 0)
    def _():
        for b, t in enumerate(toks):
            whole[b * t.shape[0] : (b + 1) * t.shape[0]] = t[...]

    contract = ((1,), (1,)) if transposed else ((1,), (0,))
    out = lax.dot_general(
        whole[...], w[...], (contract, ((), ())), preferred_element_type=jnp.float32
    )
    places = (
        (keep_a, 0), (keep_b, 0),
        (send_a, 0), (keep_b, 1),
        (keep_a, 1), (send_b, 0),
        (send_a, 1), (send_b, 1),
    )
    for at, (ref, slot) in enumerate(places):
        @pl.when(step == at)
        def _():
            ref[slot] = out.astype(ref.dtype)


def project(me, toks, w, transposed, n_row, after=()):
    rows = sum(t.shape[0] for t in toks)
    depth = toks[0].shape[1]
    wide = (w.shape[0] if transposed else w.shape[1]) // (2 * n_row)

    def block(s, idx):
        return ((idx[0] ^ (s // 2)) * 2 + s % 2, 0)

    if transposed:
        w_spec = pl.BlockSpec((wide, depth), block)
    else:
        w_spec = pl.BlockSpec((depth, wide), lambda s, idx: block(s, idx)[::-1])
    send = jax.ShapeDtypeStruct((2, rows, wide), jnp.bfloat16)
    keep = jax.ShapeDtypeStruct((2, rows, wide), jnp.float32)
    whole = jax.ShapeDtypeStruct((rows, depth), jnp.bfloat16)
    return pl.pallas_call(
        functools.partial(project_body, transposed, len(toks)),
        grid_spec=pltpu.PrefetchScalarGridSpec(
            num_scalar_prefetch=1,
            grid=(2 * n_row,),
            in_specs=[pl.BlockSpec(t.shape, lambda s, idx: (0, 0)) for t in toks]
            + [w_spec] + [hbm] * len(after),
            out_specs=[pl.BlockSpec(send.shape, lambda s, idx: (0, 0, 0))] * 4
            + [pl.BlockSpec(whole.shape, lambda s, idx: (0, 0))],
        ),
        out_shape=[send, keep, send, keep, whole],
        compiler_params=pltpu.CompilerParams(vmem_limit_bytes=vmem_bytes),
        cost_estimate=cost(2 * rows * w.size, 2 * w.size + 2 * rows * depth + 24 * rows * wide),
        name="project_back" if transposed else "project_pre",
    )(me, *toks, w, *after)


def mix_body(n_half, n_col, n_after, idx, *refs):
    hidden, w = refs[:n_half], refs[n_half]
    out, pack, total = refs[-3:]
    step = pl.program_id(0)
    for at, h in enumerate(hidden):
        @pl.when(step == at)
        def _():
            part = jnp.dot(h[...], w[...], preferred_element_type=jnp.float32)
            total[...] = part if at == 0 else total[...] + part
            if at >= 2:
                pack[at - 2] = h[...]
    @pl.when(step == n_half - 1)
    def _():
        rows = out.shape[1]
        for b in range(n_col):
            out[lax.rem(idx[1] + n_col - b, n_col)] = total[b * rows : (b + 1) * rows]


def half_spec(whole, h):
    if whole.ndim == 3:
        return pl.BlockSpec((None,) + whole.shape[1:], lambda *_: (h, 0, 0))
    return pl.BlockSpec(whole.shape, lambda *_: (0, 0))


def mix(at, halves, w, n_col, after=()):
    rows, wide = halves[0][0].shape[-2:]
    depth = w.shape[1]
    share = rows // n_col
    n_half = len(halves)
    out = jax.ShapeDtypeStruct((n_col, share, depth), jnp.float32)
    pack = jax.ShapeDtypeStruct((n_half - 2, rows, wide), jnp.bfloat16)
    return pl.pallas_call(
        functools.partial(mix_body, n_half, n_col, len(after)),
        grid_spec=pltpu.PrefetchScalarGridSpec(
            num_scalar_prefetch=1,
            grid=(n_half,),
            in_specs=[half_spec(*h) for h in halves]
            + [pl.BlockSpec((wide, depth), lambda s, idx: ((idx[0] ^ (s // 2)) * 2 + s % 2, 0))]
            + [hbm] * len(after),
            out_specs=[pl.BlockSpec(a.shape, lambda s, idx: (0, 0, 0)) for a in (out, pack)],
            scratch_shapes=[pltpu.VMEM((rows, depth), jnp.float32)],
        ),
        out_shape=[out, pack],
        compiler_params=pltpu.CompilerParams(vmem_limit_bytes=vmem_bytes),
        cost_estimate=cost(2 * rows * w.size, 2 * w.size + 4 * rows * w.shape[0] + 4 * rows * depth),
        name="mix",
    )(at, *[h[0] for h in halves], w, *after)


def late_body(keep_a, got_a, keep_b, got_b, *refs):
    out_a, out_b = refs[-2:]
    for keep, got, out in ((keep_a, got_a, out_a), (keep_b, got_b, out_b)):
        out[...] = (keep[...] + got[...].astype(jnp.float32)).astype(jnp.bfloat16)


def late_sums(keep_a, got_a, keep_b, got_b, after):
    _, rows, wide = keep_a.shape
    spec = pl.BlockSpec((None, rows, wide), lambda i: (1, 0, 0))
    out = jax.ShapeDtypeStruct((rows, wide), jnp.bfloat16)
    return pl.pallas_call(
        late_body,
        grid=(1,),
        in_specs=[spec] * 4 + [hbm] * len(after),
        out_specs=[pl.BlockSpec((rows, wide), lambda i: (0, 0))] * 2,
        out_shape=[out, out],
        compiler_params=pltpu.CompilerParams(vmem_limit_bytes=vmem_bytes),
        name="late_sums",
    )(keep_a, got_a, keep_b, got_b, *after)


def sum_of(keep_a, got_a, late_a, keep_b, got_b, late_b):
    return [
        (0, keep_a[...] + got_a[...].astype(jnp.float32) + late_a[...].astype(jnp.float32)),
        (1, keep_b[...] + got_b[...].astype(jnp.float32) + late_b[...].astype(jnp.float32)),
    ]


def activate_body(*refs):
    cs, xs, (hidden, slope, pack) = refs[12], refs[13], refs[-3:]
    wide = hidden.shape[2]
    for (h, pre), (_, back) in zip(sum_of(*refs[:6]), sum_of(*refs[6:12])):
        half = slice(h * wide, (h + 1) * wide)
        hidden[h] = pack[h] = gelu_value(pre).astype(jnp.bfloat16)
        pack[2 + h] = cs[:, half]
        slope[h] = pack[4 + h] = (back * gelu_slope(pre)).astype(jnp.bfloat16)
        pack[6 + h] = xs[:, half]


def activate(pre_parts, back_parts, c_all, x_all):
    _, rows, wide = pre_parts[0].shape
    part = rows // 4 if rows % 64 == 0 else rows
    kept = pl.BlockSpec((None, part, wide), lambda i: (0, i, 0))
    late = pl.BlockSpec((part, wide), lambda i: (i, 0))
    return pl.pallas_call(
        activate_body,
        grid=(rows // part,),
        in_specs=[kept, kept, late] * 4
        + [pl.BlockSpec((part, c_all.shape[1]), lambda i: (i, 0))] * 2,
        out_specs=[pl.BlockSpec((n, part, wide), lambda i: (0, i, 0)) for n in (2, 2, 8)],
        out_shape=[jax.ShapeDtypeStruct((n, rows, wide), jnp.bfloat16) for n in (2, 2, 8)],
        compiler_params=pltpu.CompilerParams(vmem_limit_bytes=vmem_bytes),
        name="activate",
    )(*pre_parts, *back_parts, c_all, x_all)


def stack_body(far_a, far_b, *refs):
    refs[-1][0] = far_a[...]
    refs[-1][1] = far_b[...]


def stack(far_a, far_b, after):
    rows, wide = far_a.shape
    return pl.pallas_call(
        stack_body,
        grid=(1,),
        in_specs=[pl.BlockSpec((rows, wide), lambda i: (0, 0))] * 2 + [hbm] * len(after),
        out_specs=pl.BlockSpec((2, rows, wide), lambda i: (0, 0, 0)),
        out_shape=jax.ShapeDtypeStruct((2, rows, wide), jnp.bfloat16),
        compiler_params=pltpu.CompilerParams(vmem_limit_bytes=vmem_bytes),
        name="stack",
    )(far_a, far_b, *after)


def forward_body(from_x, from_y, *refs):
    out_a, out_b = refs[-2:]
    out_a[...] = from_x[...]
    out_b[...] = from_y[...]


def forward(from_x, from_y, after):
    _, rows, wide = from_x.shape
    out = jax.ShapeDtypeStruct((rows, wide), jnp.bfloat16)
    return pl.pallas_call(
        forward_body,
        grid=(1,),
        in_specs=[pl.BlockSpec((None, rows, wide), lambda i, h=h: (h, 0, 0)) for h in range(2)]
        + [hbm] * len(after),
        out_specs=[pl.BlockSpec((rows, wide), lambda i: (0, 0))] * 2,
        out_shape=[out, out],
        compiler_params=pltpu.CompilerParams(vmem_limit_bytes=vmem_bytes),
        name="forward",
    )(from_x, from_y, *after)


def vote_of(grad, moment, scale):
    moved = (momentum_decay / vote_scale) * moment.astype(jnp.float32) + scale * grad
    return jnp.tanh(moved).astype(jnp.bfloat16)


def transposed_dot(left, right):
    return lax.dot_general(
        left, right, (((0,), (0,)), ((), ())), preferred_element_type=jnp.float32
    )


def total_of(first, second):
    return first + second


def tally_in_body(scale, idx, x0, x1, s0, s1, m0, m1, *rest):
    out = rest[-1]
    wide = s0.shape[2]
    for h in range(2):
        for c in range(0, wide, wide // 2):
            part = slice(c, c + wide // 2)
            to = slice(h * wide + c, h * wide + c + wide // 2)
            v0 = vote_of(transposed_dot(x0[...], s0[h, :, part]), m0[:, to], scale)
            v1 = vote_of(transposed_dot(x1[...], s1[h, :, part]), m1[:, to], scale)
            out[:, to] = total_of(v0, v1)


def tally_out_body(scale, idx, c0, c1, s0, s1, m0, m1, *rest):
    out = rest[-1]
    half = c1.shape[2]
    step = half // 2 if half % 256 == 0 else half
    for h in range(2):
        for c in range(0, half, step):
            part = slice(c, c + step)
            to = slice(h * half + c, h * half + c + step)
            v0 = vote_of(transposed_dot(s0[...], c0[:, to]), m0[:, to], scale)
            v1 = vote_of(transposed_dot(s1[...], c1[h, :, part]), m1[:, to], scale)
            out[:, to] = total_of(v0, v1)


def tally(kind, quarters, fixed, halves, moments, into, scale, after=(), skip=0):
    rows, cols = moments[0].shape
    n_half, (_, toks, wide) = 2 * (quarters.size - 1), halves[0].shape
    if kind == "in":
        high = wide
        grid = (n_half // 2, rows // high)
        per = wide // high
        fixed_specs = [
            pl.BlockSpec((toks, high), lambda k, i, q: (0, i)),
            pl.BlockSpec((None, toks, high), lambda k, i, q: (6 + i // per, 0, i % per)),
        ]
        pair_specs = [
            pl.BlockSpec((2, toks, wide), lambda k, i, q, b=b: (k + b, 0, 0)) for b in (0, skip)
        ]
        m_spec = pl.BlockSpec((high, 2 * wide), lambda k, i, q: (i, q[k]))
        peer_spec = pl.BlockSpec((None, high, 2 * wide), lambda k, i, q: (q[n_half // 2], i, q[k]))
        body = functools.partial(tally_in_body, scale)
        area = rows * n_half * wide
    else:
        high = wide
        per = wide // high
        grid = (n_half // 2, 2, per)
        fixed_specs = [
            pl.BlockSpec((toks, cols), lambda k, h, i, q: (0, 0)),
            pl.BlockSpec((2, toks, wide), lambda k, h, i, q: (1, 0, 0)),
        ]
        pair_specs = [pl.BlockSpec((None, toks, high), lambda k, h, i, q: (2 * k + h, 0, i))] * 2
        m_spec = pl.BlockSpec((high, cols), lambda k, h, i, q: ((2 * q[k] + h) * per + i, 0))
        peer_spec = pl.BlockSpec(
            (None, high, cols), lambda k, h, i, q: (q[n_half // 2], (2 * q[k] + h) * per + i, 0)
        )
        body = functools.partial(tally_out_body, scale)
        area = cols * n_half * wide
    old = [] if into is None else [into]
    return pl.pallas_call(
        body,
        grid_spec=pltpu.PrefetchScalarGridSpec(
            num_scalar_prefetch=1,
            grid=grid,
            in_specs=fixed_specs + pair_specs
            + [m_spec, peer_spec if moments[1].ndim == 3 else m_spec]
            + [hbm] * len(old + list(after)),
            out_specs=m_spec,
        ),
        out_shape=jax.ShapeDtypeStruct((rows, cols), jnp.bfloat16),
        input_output_aliases={7: 0} if old else {},
        compiler_params=pltpu.CompilerParams(vmem_limit_bytes=vmem_bytes),
        cost_estimate=cost(4 * toks * area, 6 * area, 2 * area),
        name="tally_" + kind,
    )(quarters, *fixed, *halves, *moments, *old, *after)


def shards_square(n_col, n_rep, patches, cotangent, w_in, w_out, moment_in, moment_out):
    n_row = 4
    if n_row * w_in.shape[0] != w_in.shape[1] or w_in.shape[0] % 256:
        return shards_plain(patches, cotangent, w_in, w_out, moment_in, moment_out)
    across_x = [(i, i ^ 1) for i in range(n_row)]
    across_y = [(i, i ^ 2) for i in range(n_row)]
    swap = [(0, 1), (1, 0)]
    row_index = lax.axis_index("row")
    me = jnp.reshape(row_index, (1,)).astype(jnp.int32)

    def to_x(a):
        return lax.ppermute(a, "row", across_x)

    def to_y(a):
        return lax.ppermute(a, "row", across_y)

    def other(a):
        return lax.ppermute(a, "rep", swap)

    def along(a, shift):
        return lax.ppermute(a, "col", [(i, (i + shift) % n_col) for i in range(n_col)])

    def f32(a):
        return a.astype(jnp.float32)

    peer = 1 - jnp.reshape(lax.axis_index("rep"), (1,)).astype(jnp.int32)

    def quarters(*ks):
        return jnp.concatenate([me ^ k for k in ks] + [peer])

    own_x, own_c = patches[0], cotangent[0]
    moment_in, moment_out = moment_in[0], moment_out[0]

    xs = [own_x] + [along(own_x, b) for b in range(1, n_col)]
    cs = [own_c] + [along(own_c, b) for b in range(1, n_col)]
    every_moment_out = lax.all_gather(moment_out, "rep")
    every_moment_in = lax.all_gather(moment_in, "rep")

    send_a, pre_a, send_b, pre_b, x_all = project(me, xs, w_in, False, n_row)
    pre_got_a, pre_got_b = to_x(send_a), to_y(send_b)
    send_a, back_a, send_b, back_b, c_all = project(me, cs, w_out, True, n_row, after=(x_all,))
    back_got_a, back_got_b = to_x(send_a), to_y(send_b)
    scale = (1.0 - momentum_decay) / (vote_scale * math.sqrt(x_all.shape[0]))

    late_a, late_b = late_sums(pre_a, pre_got_a, pre_b, pre_got_b, after=(c_all,))
    pre_late_a, pre_late_b = to_y(late_a), to_x(late_b)
    late_a, late_b = late_sums(back_a, back_got_a, back_b, back_got_b, after=(late_a,))
    back_late_a, back_late_b = to_y(late_a), to_x(late_b)

    hidden, slope, pack = activate(
        (pre_a, pre_got_a, pre_late_a, pre_b, pre_got_b, pre_late_b),
        (back_a, back_got_a, back_late_a, back_b, back_got_b, back_late_b),
        c_all,
        x_all,
    )
    pack = other(pack)
    hidden_x, hidden_y = to_x(hidden), to_y(hidden)
    slope_x, slope_y = to_x(slope), to_y(slope)

    both_c, both_out = (c_all, pack), (moment_out, every_moment_out)
    both_x, both_in = (x_all, pack), (moment_in, every_moment_in)

    tally_out = tally(
        "out", quarters(0), both_c, (hidden, pack), both_out, None, scale
    )
    near_a, near_b = forward(hidden_x, hidden_y, after=(tally_out,))
    hidden_far_a, hidden_far_b = to_y(near_a), to_x(near_b)
    tally_in = tally(
        "in", quarters(0), both_x, (slope, pack), both_in, None, scale, after=(near_a,), skip=2
    )
    far_a, far_b = forward(slope_x, slope_y, after=(tally_in,))
    slope_far_a, slope_far_b = to_y(far_a), to_x(far_b)
    column = jnp.reshape(lax.axis_index("col"), (1,)).astype(jnp.int32)
    parts, hidden_rest = mix(
        jnp.concatenate([me, column]),
        [(a, h) for a in (hidden, hidden_x, hidden_y) for h in range(2)]
        + [(hidden_far_a, 0), (hidden_far_b, 0)],
        w_out,
        n_col,
        after=(far_a,),
    )
    mixed = lax.psum_scatter(parts, "col", scatter_dimension=0, tiled=True).astype(jnp.bfloat16)
    hidden_rest_other = other(hidden_rest)
    near = jnp.concatenate([slope_x, slope_y])
    near_other = other(near)
    tally_out = tally(
        "out", quarters(1, 2, 3), both_c, (hidden_rest, hidden_rest_other), both_out, tally_out,
        scale, after=(near, far_a),
    )
    far = stack(slope_far_a, slope_far_b, after=(tally_out,))
    tally_in = tally(
        "in", quarters(1, 2), both_x, (near, near_other), both_in, tally_in, scale,
        after=(tally_out, far),
    )
    tally_in = tally("in", quarters(3), both_x, (far, other(far)), both_in, tally_in, scale)
    return mixed, tally_in, tally_out


def solution(mesh):
    in_specs = (
        P("rep", "col", "row"),
        P("rep", "col", "row"),
        P("row", "col"),
        P("col", "row"),
        P("rep", "row", "col"),
        P("rep", "col", "row"),
    )
    out_specs = (P("rep", "col", "row"), P("row", "col"), P("col", "row"))
    sizes = dict(mesh.shape)
    if sizes["row"] == 4 and sizes["rep"] == 2:
        body = functools.partial(shards_square, sizes["col"], sizes["rep"])
    else:
        body = shards_plain
    return jax.shard_map(body, mesh=mesh, in_specs=in_specs, out_specs=out_specs, check_vma=False)
```

```python
import functools
import math

import jax
import jax.numpy as jnp
from jax import lax
from jax.experimental import pallas as pl
from jax.experimental.pallas import tpu as pltpu
from jax.sharding import PartitionSpec as P

momentum_decay = 0.9
vote_scale = 0.3
vmem_bytes = 48 * 2**20
hbm = pl.BlockSpec(memory_space=pl.ANY)


def cost(flops, moved, transcendentals=0):
    return pl.CostEstimate(
        flops=int(flops), bytes_accessed=int(moved), transcendentals=int(transcendentals)
    )


def gelu_value(pre):
    return 0.5 * pre * (1.0 + lax.erf(pre * (1.0 / math.sqrt(2.0))))


def gelu_slope(pre):
    return 0.5 * (1.0 + lax.erf(pre * (1.0 / math.sqrt(2.0)))) + pre * jnp.exp(-0.5 * pre * pre) * (
        1.0 / math.sqrt(2.0 * math.pi)
    )


def shards_plain(patches, cotangent, w_in, w_out, moment_in, moment_out):
    inputs = lax.all_gather(patches[0], "col", axis=0, tiled=True)
    norm_factor = 1.0 / math.sqrt(inputs.shape[0])
    pre_share = lax.psum_scatter(
        jnp.dot(inputs, w_in, preferred_element_type=jnp.float32),
        "row",
        scatter_dimension=0,
        tiled=True,
    )
    hidden = lax.all_gather(
        gelu_value(pre_share).astype(jnp.bfloat16), "row", axis=0, tiled=True
    )
    mixed = lax.psum_scatter(
        jnp.dot(hidden, w_out, preferred_element_type=jnp.float32),
        "col",
        scatter_dimension=0,
        tiled=True,
    ).astype(jnp.bfloat16)
    grads = lax.all_gather(cotangent[0], "col", axis=0, tiled=True)
    back_share = lax.psum_scatter(
        lax.dot_general(
            grads, w_out, (((1,), (1,)), ((), ())), preferred_element_type=jnp.float32
        ).astype(jnp.bfloat16),
        "row",
        scatter_dimension=0,
        tiled=True,
    ).astype(jnp.float32)
    slope_share = (back_share * gelu_slope(pre_share)).astype(jnp.bfloat16)
    slope = lax.all_gather(slope_share, "row", axis=0, tiled=True)

    def votes(moment, left, right):
        grad = norm_factor * lax.dot_general(
            left, right, (((0,), (0,)), ((), ())), preferred_element_type=jnp.float32
        )
        moved = momentum_decay * moment.astype(jnp.float32) + (1.0 - momentum_decay) * grad
        vote = jnp.tanh(moved / vote_scale).astype(jnp.bfloat16)
        return lax.psum(vote, "rep").astype(jnp.float32).astype(jnp.bfloat16)

    return (
        mixed[None],
        votes(moment_in[0], inputs, slope),
        votes(moment_out[0], hidden, grads),
    )


def project_body(transposed, n_tok, idx, *refs):
    toks, w, (send_a, keep_a, send_b, keep_b, whole) = refs[:n_tok], refs[n_tok], refs[-5:]
    step = pl.program_id(0)

    @pl.when(step == 0)
    def _():
        for b, t in enumerate(toks):
            whole[b * t.shape[0] : (b + 1) * t.shape[0]] = t[...]

    contract = ((1,), (1,)) if transposed else ((1,), (0,))
    out = lax.dot_general(
        whole[...], w[...], (contract, ((), ())), preferred_element_type=jnp.float32
    )
    places = (
        (keep_a, 0), (keep_b, 0),
        (send_a, 0), (keep_b, 1),
        (keep_a, 1), (send_b, 0),
        (send_a, 1), (send_b, 1),
    )
    for at, (ref, slot) in enumerate(places):
        @pl.when(step == at)
        def _():
            ref[slot] = out.astype(ref.dtype)


def project(me, toks, w, transposed, n_row, after=()):
    rows = sum(t.shape[0] for t in toks)
    depth = toks[0].shape[1]
    wide = (w.shape[0] if transposed else w.shape[1]) // (2 * n_row)

    def block(s, idx):
        return ((idx[0] ^ (s // 2)) * 2 + s % 2, 0)

    if transposed:
        w_spec = pl.BlockSpec((wide, depth), block)
    else:
        w_spec = pl.BlockSpec((depth, wide), lambda s, idx: block(s, idx)[::-1])
    send = jax.ShapeDtypeStruct((2, rows, wide), jnp.bfloat16)
    keep = jax.ShapeDtypeStruct((2, rows, wide), jnp.float32)
    whole = jax.ShapeDtypeStruct((rows, depth), jnp.bfloat16)
    return pl.pallas_call(
        functools.partial(project_body, transposed, len(toks)),
        grid_spec=pltpu.PrefetchScalarGridSpec(
            num_scalar_prefetch=1,
            grid=(2 * n_row,),
            in_specs=[pl.BlockSpec(t.shape, lambda s, idx: (0, 0)) for t in toks]
            + [w_spec] + [hbm] * len(after),
            out_specs=[pl.BlockSpec(send.shape, lambda s, idx: (0, 0, 0))] * 4
            + [pl.BlockSpec(whole.shape, lambda s, idx: (0, 0))],
        ),
        out_shape=[send, keep, send, keep, whole],
        compiler_params=pltpu.CompilerParams(vmem_limit_bytes=vmem_bytes),
        cost_estimate=cost(2 * rows * w.size, 2 * w.size + 2 * rows * depth + 24 * rows * wide),
        name="project_back" if transposed else "project_pre",
    )(me, *toks, w, *after)


def mix_body(n_half, n_col, n_after, idx, *refs):
    hidden, w = refs[:n_half], refs[n_half]
    out, pack, total = refs[-3:]
    step = pl.program_id(0)
    for at, h in enumerate(hidden):
        @pl.when(step == at)
        def _():
            part = jnp.dot(h[...], w[...], preferred_element_type=jnp.float32)
            total[...] = part if at == 0 else total[...] + part
            if at >= 2:
                pack[at - 2] = h[...]
    @pl.when(step == n_half - 1)
    def _():
        rows = out.shape[1]
        for b in range(n_col):
            out[lax.rem(idx[1] + n_col - b, n_col)] = total[b * rows : (b + 1) * rows]


def half_spec(whole, h):
    if whole.ndim == 3:
        return pl.BlockSpec((None,) + whole.shape[1:], lambda *_: (h, 0, 0))
    return pl.BlockSpec(whole.shape, lambda *_: (0, 0))


def mix(at, halves, w, n_col, after=()):
    rows, wide = halves[0][0].shape[-2:]
    depth = w.shape[1]
    share = rows // n_col
    n_half = len(halves)
    out = jax.ShapeDtypeStruct((n_col, share, depth), jnp.float32)
    pack = jax.ShapeDtypeStruct((n_half - 2, rows, wide), jnp.bfloat16)
    return pl.pallas_call(
        functools.partial(mix_body, n_half, n_col, len(after)),
        grid_spec=pltpu.PrefetchScalarGridSpec(
            num_scalar_prefetch=1,
            grid=(n_half,),
            in_specs=[half_spec(*h) for h in halves]
            + [pl.BlockSpec((wide, depth), lambda s, idx: ((idx[0] ^ (s // 2)) * 2 + s % 2, 0))]
            + [hbm] * len(after),
            out_specs=[pl.BlockSpec(a.shape, lambda s, idx: (0, 0, 0)) for a in (out, pack)],
            scratch_shapes=[pltpu.VMEM((rows, depth), jnp.float32)],
        ),
        out_shape=[out, pack],
        compiler_params=pltpu.CompilerParams(vmem_limit_bytes=vmem_bytes),
        cost_estimate=cost(2 * rows * w.size, 2 * w.size + 4 * rows * w.shape[0] + 4 * rows * depth),
        name="mix",
    )(at, *[h[0] for h in halves], w, *after)


def late_body(keep_a, got_a, keep_b, got_b, *refs):
    out_a, out_b = refs[-2:]
    for keep, got, out in ((keep_a, got_a, out_a), (keep_b, got_b, out_b)):
        out[...] = (keep[...] + got[...].astype(jnp.float32)).astype(jnp.bfloat16)


def late_sums(keep_a, got_a, keep_b, got_b, after):
    _, rows, wide = keep_a.shape
    spec = pl.BlockSpec((None, rows, wide), lambda i: (1, 0, 0))
    out = jax.ShapeDtypeStruct((rows, wide), jnp.bfloat16)
    return pl.pallas_call(
        late_body,
        grid=(1,),
        in_specs=[spec] * 4 + [hbm] * len(after),
        out_specs=[pl.BlockSpec((rows, wide), lambda i: (0, 0))] * 2,
        out_shape=[out, out],
        compiler_params=pltpu.CompilerParams(vmem_limit_bytes=vmem_bytes),
        name="late_sums",
    )(keep_a, got_a, keep_b, got_b, *after)


def sum_of(keep_a, got_a, late_a, keep_b, got_b, late_b):
    return [
        (0, keep_a[...] + got_a[...].astype(jnp.float32) + late_a[...].astype(jnp.float32)),
        (1, keep_b[...] + got_b[...].astype(jnp.float32) + late_b[...].astype(jnp.float32)),
    ]


def activate_body(*refs):
    cs, xs, (hidden, slope, pack) = refs[12], refs[13], refs[-3:]
    wide = hidden.shape[2]
    for (h, pre), (_, back) in zip(sum_of(*refs[:6]), sum_of(*refs[6:12])):
        half = slice(h * wide, (h + 1) * wide)
        hidden[h] = pack[h] = gelu_value(pre).astype(jnp.bfloat16)
        pack[2 + h] = cs[:, half]
        slope[h] = pack[4 + h] = (back * gelu_slope(pre)).astype(jnp.bfloat16)
        pack[6 + h] = xs[:, half]


def activate(pre_parts, back_parts, c_all, x_all):
    _, rows, wide = pre_parts[0].shape
    part = rows // 4 if rows % 64 == 0 else rows
    kept = pl.BlockSpec((None, part, wide), lambda i: (0, i, 0))
    late = pl.BlockSpec((part, wide), lambda i: (i, 0))
    return pl.pallas_call(
        activate_body,
        grid=(rows // part,),
        in_specs=[kept, kept, late] * 4
        + [pl.BlockSpec((part, c_all.shape[1]), lambda i: (i, 0))] * 2,
        out_specs=[pl.BlockSpec((n, part, wide), lambda i: (0, i, 0)) for n in (2, 2, 8)],
        out_shape=[jax.ShapeDtypeStruct((n, rows, wide), jnp.bfloat16) for n in (2, 2, 8)],
        compiler_params=pltpu.CompilerParams(vmem_limit_bytes=vmem_bytes),
        name="activate",
    )(*pre_parts, *back_parts, c_all, x_all)


def stack_body(far_a, far_b, *refs):
    refs[-1][0] = far_a[...]
    refs[-1][1] = far_b[...]


def stack(far_a, far_b, after):
    rows, wide = far_a.shape
    return pl.pallas_call(
        stack_body,
        grid=(1,),
        in_specs=[pl.BlockSpec((rows, wide), lambda i: (0, 0))] * 2 + [hbm] * len(after),
        out_specs=pl.BlockSpec((2, rows, wide), lambda i: (0, 0, 0)),
        out_shape=jax.ShapeDtypeStruct((2, rows, wide), jnp.bfloat16),
        compiler_params=pltpu.CompilerParams(vmem_limit_bytes=vmem_bytes),
        name="stack",
    )(far_a, far_b, *after)


def forward_body(from_x, from_y, *refs):
    out_a, out_b = refs[-2:]
    out_a[...] = from_x[...]
    out_b[...] = from_y[...]


def forward(from_x, from_y, after):
    _, rows, wide = from_x.shape
    out = jax.ShapeDtypeStruct((rows, wide), jnp.bfloat16)
    return pl.pallas_call(
        forward_body,
        grid=(1,),
        in_specs=[pl.BlockSpec((None, rows, wide), lambda i, h=h: (h, 0, 0)) for h in range(2)]
        + [hbm] * len(after),
        out_specs=[pl.BlockSpec((rows, wide), lambda i: (0, 0))] * 2,
        out_shape=[out, out],
        compiler_params=pltpu.CompilerParams(vmem_limit_bytes=vmem_bytes),
        name="forward",
    )(from_x, from_y, *after)


def vote_of(grad, moment, scale):
    moved = (momentum_decay / vote_scale) * moment.astype(jnp.float32) + scale * grad
    return jnp.tanh(moved).astype(jnp.bfloat16)


def transposed_dot(left, right):
    return lax.dot_general(
        left, right, (((0,), (0,)), ((), ())), preferred_element_type=jnp.float32
    )


def total_of(first, second):
    return first + second


def tally_in_body(scale, idx, x0, x1, s0, s1, m0, m1, *rest):
    out = rest[-1]
    wide = s0.shape[2]
    for h in range(2):
        for c in range(0, wide, wide // 2):
            part = slice(c, c + wide // 2)
            to = slice(h * wide + c, h * wide + c + wide // 2)
            v0 = vote_of(transposed_dot(x0[...], s0[h, :, part]), m0[:, to], scale)
            v1 = vote_of(transposed_dot(x1[...], s1[h, :, part]), m1[:, to], scale)
            out[:, to] = total_of(v0, v1)


def tally_out_body(scale, idx, c0, c1, s0, s1, m0, m1, *rest):
    out = rest[-1]
    half = c1.shape[2]
    step = half // 2 if half % 256 == 0 else half
    for h in range(2):
        for c in range(0, half, step):
            part = slice(c, c + step)
            to = slice(h * half + c, h * half + c + step)
            v0 = vote_of(transposed_dot(s0[...], c0[:, to]), m0[:, to], scale)
            v1 = vote_of(transposed_dot(s1[...], c1[h, :, part]), m1[:, to], scale)
            out[:, to] = total_of(v0, v1)


def tally(kind, quarters, fixed, halves, moments, into, scale, after=(), skip=0):
    rows, cols = moments[0].shape
    n_half, (_, toks, wide) = 2 * (quarters.size - 1), halves[0].shape
    if kind == "in":
        high = wide
        grid = (n_half // 2, rows // high)
        per = wide // high
        fixed_specs = [
            pl.BlockSpec((toks, high), lambda k, i, q: (0, i)),
            pl.BlockSpec((None, toks, high), lambda k, i, q: (6 + i // per, 0, i % per)),
        ]
        pair_specs = [
            pl.BlockSpec((2, toks, wide), lambda k, i, q, b=b: (k + b, 0, 0)) for b in (0, skip)
        ]
        m_spec = pl.BlockSpec((high, 2 * wide), lambda k, i, q: (i, q[k]))
        peer_spec = pl.BlockSpec((None, high, 2 * wide), lambda k, i, q: (q[n_half // 2], i, q[k]))
        body = functools.partial(tally_in_body, scale)
        area = rows * n_half * wide
    else:
        high = wide
        per = wide // high
        grid = (n_half // 2, 2, per)
        fixed_specs = [
            pl.BlockSpec((toks, cols), lambda k, h, i, q: (0, 0)),
            pl.BlockSpec((2, toks, wide), lambda k, h, i, q: (1, 0, 0)),
        ]
        pair_specs = [pl.BlockSpec((None, toks, high), lambda k, h, i, q: (2 * k + h, 0, i))] * 2
        m_spec = pl.BlockSpec((high, cols), lambda k, h, i, q: ((2 * q[k] + h) * per + i, 0))
        peer_spec = pl.BlockSpec(
            (None, high, cols), lambda k, h, i, q: (q[n_half // 2], (2 * q[k] + h) * per + i, 0)
        )
        body = functools.partial(tally_out_body, scale)
        area = cols * n_half * wide
    old = [] if into is None else [into]
    return pl.pallas_call(
        body,
        grid_spec=pltpu.PrefetchScalarGridSpec(
            num_scalar_prefetch=1,
            grid=grid,
            in_specs=fixed_specs + pair_specs
            + [m_spec, peer_spec if moments[1].ndim == 3 else m_spec]
            + [hbm] * len(old + list(after)),
            out_specs=m_spec,
        ),
        out_shape=jax.ShapeDtypeStruct((rows, cols), jnp.bfloat16),
        input_output_aliases={7: 0} if old else {},
        compiler_params=pltpu.CompilerParams(vmem_limit_bytes=vmem_bytes),
        cost_estimate=cost(4 * toks * area, 6 * area, 2 * area),
        name="tally_" + kind,
    )(quarters, *fixed, *halves, *moments, *old, *after)


def shards_square(n_col, n_rep, patches, cotangent, w_in, w_out, moment_in, moment_out):
    n_row = 4
    if n_row * w_in.shape[0] != w_in.shape[1] or w_in.shape[0] % 256:
        return shards_plain(patches, cotangent, w_in, w_out, moment_in, moment_out)
    across_x = [(i, i ^ 1) for i in range(n_row)]
    across_y = [(i, i ^ 2) for i in range(n_row)]
    swap = [(0, 1), (1, 0)]
    row_index = lax.axis_index("row")
    me = jnp.reshape(row_index, (1,)).astype(jnp.int32)

    def to_x(a):
        return lax.ppermute(a, "row", across_x)

    def to_y(a):
        return lax.ppermute(a, "row", across_y)

    def other(a):
        return lax.ppermute(a, "rep", swap)

    def along(a, shift):
        return lax.ppermute(a, "col", [(i, (i + shift) % n_col) for i in range(n_col)])

    def f32(a):
        return a.astype(jnp.float32)

    peer = 1 - jnp.reshape(lax.axis_index("rep"), (1,)).astype(jnp.int32)

    def quarters(*ks):
        return jnp.concatenate([me ^ k for k in ks] + [peer])

    own_x, own_c = patches[0], cotangent[0]
    moment_in, moment_out = moment_in[0], moment_out[0]

    xs = [own_x] + [along(own_x, b) for b in range(1, n_col)]
    cs = [own_c] + [along(own_c, b) for b in range(1, n_col)]
    every_moment_out = other(moment_out)
    every_moment_in = other(moment_in)

    send_a, pre_a, send_b, pre_b, x_all = project(me, xs, w_in, False, n_row)
    pre_got_a, pre_got_b = to_x(send_a), to_y(send_b)
    send_a, back_a, send_b, back_b, c_all = project(me, cs, w_out, True, n_row, after=(x_all,))
    back_got_a, back_got_b = to_x(send_a), to_y(send_b)
    scale = (1.0 - momentum_decay) / (vote_scale * math.sqrt(x_all.shape[0]))

    late_a, late_b = late_sums(pre_a, pre_got_a, pre_b, pre_got_b, after=(c_all,))
    pre_late_a, pre_late_b = to_y(late_a), to_x(late_b)
    late_a, late_b = late_sums(back_a, back_got_a, back_b, back_got_b, after=(late_a,))
    back_late_a, back_late_b = to_y(late_a), to_x(late_b)

    hidden, slope, pack = activate(
        (pre_a, pre_got_a, pre_late_a, pre_b, pre_got_b, pre_late_b),
        (back_a, back_got_a, back_late_a, back_b, back_got_b, back_late_b),
        c_all,
        x_all,
    )
    pack = other(pack)
    hidden_x, hidden_y = to_x(hidden), to_y(hidden)
    slope_x, slope_y = to_x(slope), to_y(slope)

    both_c, both_out = (c_all, pack), (moment_out, every_moment_out)
    both_x, both_in = (x_all, pack), (moment_in, every_moment_in)

    tally_out = tally(
        "out", quarters(0), both_c, (hidden, pack), both_out, None, scale
    )
    near_a, near_b = forward(hidden_x, hidden_y, after=(tally_out,))
    hidden_far_a, hidden_far_b = to_y(near_a), to_x(near_b)
    tally_in = tally(
        "in", quarters(0), both_x, (slope, pack), both_in, None, scale, after=(near_a,), skip=2
    )
    far_a, far_b = forward(slope_x, slope_y, after=(tally_in,))
    slope_far_a, slope_far_b = to_y(far_a), to_x(far_b)
    column = jnp.reshape(lax.axis_index("col"), (1,)).astype(jnp.int32)
    parts, hidden_rest = mix(
        jnp.concatenate([me, column]),
        [(a, h) for a in (hidden, hidden_x, hidden_y) for h in range(2)]
        + [(hidden_far_a, 0), (hidden_far_b, 0)],
        w_out,
        n_col,
        after=(far_a,),
    )
    mixed = lax.dynamic_index_in_dim(parts, column[0], 0)
    for b in range(1, n_col):
        part = lax.dynamic_index_in_dim(parts, (column[0] + n_col - b) % n_col, 0)
        mixed = mixed + f32(along(part.astype(jnp.bfloat16), -b))
    mixed = mixed.astype(jnp.bfloat16)
    hidden_rest_other = other(hidden_rest)
    near = jnp.concatenate([slope_x, slope_y])
    near_other = other(near)
    tally_out = tally(
        "out", quarters(1, 2, 3), both_c, (hidden_rest, hidden_rest_other), both_out, tally_out,
        scale, after=(near, far_a),
    )
    far = stack(slope_far_a, slope_far_b, after=(tally_out,))
    tally_in = tally(
        "in", quarters(1, 2), both_x, (near, near_other), both_in, tally_in, scale,
        after=(tally_out, far),
    )
    tally_in = tally("in", quarters(3), both_x, (far, other(far)), both_in, tally_in, scale)
    return mixed, tally_in, tally_out


def solution(mesh):
    in_specs = (
        P("rep", "col", "row"),
        P("rep", "col", "row"),
        P("row", "col"),
        P("col", "row"),
        P("rep", "row", "col"),
        P("rep", "col", "row"),
    )
    out_specs = (P("rep", "col", "row"), P("row", "col"), P("col", "row"))
    sizes = dict(mesh.shape)
    if sizes["row"] == 4 and sizes["rep"] == 2:
        body = functools.partial(shards_square, sizes["col"], sizes["rep"])
    else:
        body = shards_plain
    return jax.shard_map(body, mesh=mesh, in_specs=in_specs, out_specs=out_specs, check_vma=False)
```
